32 devices in a mesh: grp: 2 (over y), row: 4 (over z), col: 2 (over x), rep: 2 (over core).
Axes of the slice: x: 2, y: 2, z: 4, core: 2. Of those that a mesh axis runs over, the one named last changes fastest.
Arguments:
- features: bfloat16 [4096, 256], P(('grp', 'row', 'col', 'rep')), parts along dimension 0, may hold values from -6 to 6
- cotangent: bfloat16 [4096, 256], P(('grp', 'row', 'col', 'rep')), parts along dimension 0, may hold values from -6 to 6
- weight: bfloat16 [256, 256], replicated, may hold values from -0.375 to 0.375
- bias: float32 [256], replicated, may hold values from -3 to 3
- tile_values: bfloat16 [8, 4, 16, 128, 128], P(('grp', 'row'), ('col', 'rep')), parts along dimension 0, may hold values from -0.3125 to 0.3125
- tile_rows: int32 [8, 4, 16], P(('grp', 'row'), ('col', 'rep')), parts along dimension 0, may hold values from 0 to 3, as said below
- tile_cols: int32 [8, 4, 16], P(('grp', 'row'), ('col', 'rep')), parts along dimension 0, may hold values from 0 to 3
- tile_counts: int32 [8, 4], P(('grp', 'row'), ('col', 'rep')), parts along dimension 0, may hold values from 1 to 16, as said below
Outputs:
- activated: bfloat16 [4096, 256], P(('grp', 'row', 'col', 'rep')), parts along dimension 0
- grad_features: bfloat16 [4096, 256], P(('grp', 'row', 'col', 'rep')), parts along dimension 0
- grad_weight: float32 [512, 256], P('grp'), parts along dimension 0
The draws below stay inside these ranges and needn't reach their ends.
There are 2 independent parts, one for each index of `grp`. The reference program is written for one: setup_inputs(seed, part) draws one part's arguments, and reference() takes and returns one part's arrays. A program takes and returns all parts, laid end to end along the dimension named above; an argument that names none is the same for every part. Nothing has to cross between parts.
Inputs may be any that keep to these rules, and one draw needn't show every extreme that they name: Within one block the pairs (tile_rows, tile_cols) of the listed tiles are distinct. Only the first tile_counts[r, b] listed tiles of a block are nonzero; the rest are ignored. Some block holds exactly 16 tiles in every draw.
All inputs are finite; a program needn't handle non-finite values.
Results may differ from the reference program's by a relative error of at most 0.015.
Values may be sent and summed in bfloat16 or wider, within the bound.
A program may use at most 128 MiB of HBM per device.

```python
import math
import jax
import jax.numpy as jnp
from jax import lax

F = 256
TILE = 128
P_SIZE = 128
NCB = 4
TR = 4
TC = 4
MAXT = 16
NODES = 2048
N_ROW = 4
N_COL = 2
N_REP = 2


def tile_layout(key):
    blocks = N_ROW * N_COL * N_REP
    keys = jax.random.split(key, blocks)

    def one_block(block_key):
        return jax.random.permutation(block_key, TR * TC)[:MAXT]
    picks = jax.vmap(one_block)(keys)
    return picks.reshape(N_ROW, N_COL * N_REP, MAXT).astype(jnp.int32)


def draw_tile_rows(key, part):
    picks = tile_layout(key)
    return (picks // TC).astype(jnp.int32)


def draw_tile_cols(key, part):
    picks = tile_layout(key)
    return (picks % TC).astype(jnp.int32)


def draw_tile_counts(key, part):
    key = jax.random.fold_in(key, 3)
    blocks = N_ROW * N_COL * N_REP
    raw = jax.random.randint(jax.random.fold_in(key, 11), (blocks,), 0, MAXT).astype(jnp.int32)
    counts = 1 + raw * (raw + MAXT) // (2 * MAXT)
    chosen = jax.random.randint(jax.random.fold_in(key, 12), (), 0, blocks).astype(jnp.int32)
    counts = jnp.where(jnp.arange(blocks, dtype=jnp.int32) == chosen, MAXT, counts)
    return counts.reshape(N_ROW, N_COL * N_REP).astype(jnp.int32)


def block_levels(own_key, dims, cuts, smallest, top_value):
    def one(axis_at, blocks):
        steps = jax.random.uniform(jax.random.fold_in(jax.random.fold_in(own_key, 6), axis_at), (blocks,), jnp.float32, smallest / len(cuts), top_value / len(cuts))
        return jnp.repeat(jnp.exp(steps), dims[axis_at] // blocks).reshape((-1,) + (1,) * (len(dims) - axis_at - 1))

    gain = one(*cuts[0])
    for cut in cuts[1:]:
        gain = gain * one(*cut)
    return gain


def centred(key, dims, scale, most, cuts=(), kind=jnp.bfloat16):
    array = scale * jax.random.normal(key, dims, jnp.float32)
    if cuts:
        array = array * block_levels(key, dims, cuts, -0.22, 0.18)
    return jnp.clip(array, -most, most).astype(kind)


def setup_inputs(seed: int = 0, part: int = 0) -> dict:
    arg_keys = jax.random.split(jax.random.key(seed), 9)
    part_keys = jax.random.split(jax.random.fold_in(arg_keys[8], part), 9)
    return {
        "features": centred(part_keys[0], (NODES, F), 1.0, 6.0, ((0, 16),)),
        "cotangent": centred(part_keys[1], (NODES, F), 1.0, 6.0, ((0, 16),)),
        "weight": centred(arg_keys[2], (F, F), F ** -0.5, 0.375),
        "bias": centred(arg_keys[3], (F,), 0.5, 3.0, (), jnp.float32),
        "tile_values": centred(part_keys[4], (N_ROW, NCB, MAXT, TILE, TILE), (3 * TILE) ** -0.5, 0.3125, ((0, 4), (1, 4))),
        "tile_rows": draw_tile_rows(jax.random.fold_in(jax.random.fold_in(arg_keys[8], part), 71), part),
        "tile_cols": draw_tile_cols(jax.random.fold_in(jax.random.fold_in(arg_keys[8], part), 71), part),
        "tile_counts": draw_tile_counts(jax.random.fold_in(jax.random.fold_in(arg_keys[8], part), 71), part),
    }


def onehot_rows(ids, count, width):
    live = jnp.arange(ids.shape[0]) < count
    hit = (ids[:, None] == jnp.arange(width)[None, :]) & live[:, None]
    return hit.astype(jnp.float32)

def forward_block(values, rows, cols, count, section):
    picked = section.reshape(TC, TILE, F)[cols]
    prod = jnp.einsum('tab,tbf->taf', values.astype(jnp.float32), picked.astype(jnp.float32), precision=lax.Precision.HIGHEST)
    table = onehot_rows(rows, count, TR)
    summed = jnp.einsum('ti,taf->iaf', table, prod, precision=lax.Precision.HIGHEST)
    return summed.reshape(TR * TILE, F)

def transposed_block(values, rows, cols, count, grads):
    picked = grads.reshape(TR, TILE, F)[rows]
    prod = jnp.einsum('tab,taf->tbf', values.astype(jnp.float32), picked.astype(jnp.float32), precision=lax.Precision.HIGHEST)
    table = onehot_rows(cols, count, TC)
    summed = jnp.einsum('tj,tbf->jbf', table, prod, precision=lax.Precision.HIGHEST)
    return summed.reshape(TC * TILE, F)

def reference(features, cotangent, weight, bias, tile_values, tile_rows, tile_cols, tile_counts):
    xw = jnp.dot(features, weight, preferred_element_type=jnp.float32).astype(jnp.bfloat16)
    pieces = xw.reshape(N_ROW, NCB, P_SIZE, F)

    def row_block(rindex):
        acc = jnp.zeros((TR * TILE, F), jnp.float32)
        for bindex in range(NCB):
            section = pieces[:, bindex].reshape(N_ROW * P_SIZE, F)
            acc = acc + forward_block(tile_values[rindex, bindex], tile_rows[rindex, bindex], tile_cols[rindex, bindex], tile_counts[rindex, bindex], section)
        return acc
    aggregated = lax.map(row_block, jnp.arange(N_ROW, dtype=jnp.int32))
    pre = aggregated.reshape(NODES, F) + bias[None, :]
    activated = jax.nn.silu(pre).astype(jnp.bfloat16)
    sig = jax.nn.sigmoid(pre)
    grad_pre = (cotangent.astype(jnp.float32) * sig * (1.0 + pre * (1.0 - sig))).astype(jnp.bfloat16)
    row_grads = grad_pre.reshape(N_ROW, NCB * P_SIZE, F)

    def column_block(bindex):

        def add_term(rindex, acc):
            term = transposed_block(tile_values[rindex, bindex], tile_rows[rindex, bindex], tile_cols[rindex, bindex], tile_counts[rindex, bindex], row_grads[rindex])
            rounded = lax.optimization_barrier(term.astype(jnp.bfloat16))
            return acc + rounded.astype(jnp.float32)
        return lax.fori_loop(0, N_ROW, add_term, jnp.zeros((N_ROW * P_SIZE, F), jnp.float32))
    sums = lax.map(column_block, jnp.arange(NCB, dtype=jnp.int32))
    grad_xw = sums.reshape(NCB, N_ROW, P_SIZE, F).transpose(1, 0, 2, 3).reshape(NODES, F).astype(jnp.bfloat16)
    grad_features = jnp.dot(grad_xw, weight.T, preferred_element_type=jnp.float32).astype(jnp.bfloat16)
    grad_weight = jnp.dot(features.T, grad_xw, preferred_element_type=jnp.float32) * (1.0 / math.sqrt(NODES))
    return (activated, grad_features, grad_weight)
```

```python
import functools
import math

import jax
import jax.numpy as jnp
from jax import lax
from jax.experimental import pallas as pl
from jax.experimental.pallas import tpu as pltpu
from jax.sharding import PartitionSpec as P

HALVES = 2
BF = jnp.bfloat16
F32 = jnp.float32


def kernel(
    sizes,
    rows_ref,
    cols_ref,
    count_ref,
    feat_hbm,
    cot_hbm,
    weight_hbm,
    bias_hbm,
    vals_hbm,
    act_ref,
    gf_ref,
    gw_ref,
    vals,
    dense,
    dense_t,
    weight,
    bias,
    cot,
    feats,
    part,
    part_in,
    own_h,
    all_h,
    term,
    term_in,
    gw_own,
    gw_in,
    gw_sum,
    gw_slice_in,
    gw_slices,
    gw_all,
    local_sem,
    feat_send,
    feat_recv,
    part_send,
    part_recv,
    h_send,
    h_recv,
    term_send,
    term_recv,
    gw1_send,
    gw1_recv,
    gw2_send,
    gw2_recv,
    gw3_send,
    gw3_recv,
    gw4_send,
    gw4_recv,
):
    n_row, n_col, n_rep, n_tiles, row_tiles, col_tiles, tile, wide, scale = sizes
    n_blk = n_col * n_rep
    half = wide // HALVES
    me_r = lax.axis_index("row")
    me_c = lax.axis_index("col")
    me_p = lax.axis_index("rep")
    me_b = me_c * n_rep + me_p

    def row_to(k):
        return lax.rem(me_r + k, n_row)

    def blk_to(k):
        return lax.rem(me_b + k, n_blk)

    def row_dev(r):
        return {"row": r}

    def blk_dev(b):
        return {"col": b // n_rep, "rep": lax.rem(b, n_rep)}

    def remote(src, dst, send, recv, dev):
        return pltpu.make_async_remote_copy(
            src_ref=src,
            dst_ref=dst,
            send_sem=send,
            recv_sem=recv,
            device_id=dev,
            device_id_type=pl.DeviceIdType.MESH,
        )

    def cut(ref, h):
        return ref.at[:, pl.ds(h * half, half)]

    own_feats = [
        pltpu.make_async_copy(cut(feat_hbm, h), feats.at[h, me_r], local_sem.at[4 + h])
        for h in range(HALVES)
    ]
    load_vals = pltpu.make_async_copy(vals_hbm, vals, local_sem.at[0])
    load_weight = pltpu.make_async_copy(weight_hbm, weight, local_sem.at[1])
    load_bias = pltpu.make_async_copy(bias_hbm, bias, local_sem.at[2])
    load_cot = pltpu.make_async_copy(cot_hbm, cot, local_sem.at[3])
    for c in own_feats:
        c.start()
    load_vals.start()
    load_weight.start()
    load_bias.start()
    load_cot.start()

    barrier = pltpu.get_barrier_semaphore()
    for k in range(1, n_row):
        pl.semaphore_signal(
            barrier, inc=1, device_id=row_dev(row_to(k)), device_id_type=pl.DeviceIdType.MESH
        )
    for k in range(1, n_blk):
        pl.semaphore_signal(
            barrier, inc=1, device_id=blk_dev(blk_to(k)), device_id_type=pl.DeviceIdType.MESH
        )
    pl.semaphore_wait(barrier, n_row + n_blk - 2)

    sends = []
    for h in range(HALVES):
        for k in range(1, n_row):
            c = remote(
                cut(feat_hbm, h),
                feats.at[h, me_r],
                feat_send.at[h, k],
                feat_recv.at[h, me_r],
                row_dev(row_to(k)),
            )
            c.start()
            sends.append(c)

    load_vals.wait()
    count = count_ref[0]

    def code_of(t):
        return jnp.where(t < count, rows_ref[t] * col_tiles + cols_ref[t], -1)

    small = n_tiles * row_tiles * col_tiles <= 256
    codes = [code_of(t) for t in range(n_tiles)] if small else None

    def place(p, i, j):
        if small:
            idx = jnp.int32(-1)
            for t in range(n_tiles):
                idx = jnp.where(codes[t] == p, t, idx)
        else:
            idx = lax.fori_loop(
                0,
                n_tiles,
                lambda t, cur: jnp.where(code_of(t) == p, t, cur),
                jnp.int32(-1),
            )
        got = vals[jnp.maximum(idx, 0)]
        got = jnp.where(idx >= 0, got, jnp.zeros_like(got))
        dense[pl.ds(i * tile, tile), pl.ds(j * tile, tile)] = got
        dense_t[pl.ds(j * tile, tile), pl.ds(i * tile, tile)] = got.T

    if small:
        for p in range(row_tiles * col_tiles):
            place(p, p // col_tiles, p % col_tiles)
    else:

        def step(p, carry):
            i = p // col_tiles
            place(p, pl.multiple_of(i, 1), p - i * col_tiles)
            return carry

        lax.fori_loop(0, row_tiles * col_tiles, step, 0)

    for h in range(HALVES):
        own_feats[h].wait()
        for k in range(1, n_row):
            src = row_to(k)
            remote(
                feats.at[h, src], feats.at[h, src], feat_send.at[h, k], feat_recv.at[h, src], row_dev(src)
            ).wait_recv()
        section = feats[h].reshape(n_row * tile, half)
        part[h] = jnp.dot(dense[...], section, preferred_element_type=F32).astype(BF)
        for k in range(n_blk - 1, 0, -1):
            b = blk_to(k)
            c = remote(
                part.at[h, pl.ds(pl.multiple_of(b * tile, tile), tile)],
                part_in.at[h, k],
                part_send.at[h, k],
                part_recv.at[h, k],
                blk_dev(b),
            )
            c.start()
            sends.append(c)

    load_weight.wait()
    load_bias.wait()
    load_cot.wait()
    pre = jnp.broadcast_to(bias[...], (tile, wide))
    agg = []
    for h in range(HALVES):
        total = part[h, pl.ds(pl.multiple_of(me_b * tile, tile), tile)].astype(F32)
        for k in range(1, n_blk):
            remote(
                part_in.at[h, k], part_in.at[h, k], part_send.at[h, k], part_recv.at[h, k], blk_dev(blk_to(k))
            ).wait_recv()
            total = total + part_in[h, k].astype(F32)
        total = total.astype(BF)
        agg.append(total)
        pre = pre + jnp.dot(total, weight[pl.ds(h * half, half), :], preferred_element_type=F32)

    sig = jax.nn.sigmoid(pre)
    grad = (cot[...].astype(F32) * sig * (1.0 + pre * (1.0 - sig))).astype(BF)
    for h in range(HALVES):
        piece = lax.dot_general(
            grad,
            weight[pl.ds(h * half, half), :],
            (((1,), (1,)), ((), ())),
            preferred_element_type=F32,
        ).astype(BF)
        own_h[h] = piece
        all_h[h, me_b] = piece
        for k in range(n_blk - 1, 0, -1):
            c = remote(
                own_h.at[h],
                all_h.at[h, me_b],
                h_send.at[h, k],
                h_recv.at[h, me_b],
                blk_dev(blk_to(k)),
            )
            c.start()
            sends.append(c)

    act_ref[...] = (pre * sig).astype(BF)

    rows1 = wide // n_blk
    for h in range(HALVES):
        gw_own[pl.ds(h * half, half), :] = (
            lax.dot_general(agg[h], grad, (((0,), (0,)), ((), ())), preferred_element_type=F32) * scale
        ).astype(BF)
    for k in range(1, n_blk):
        b = blk_to(k)
        c = remote(
            gw_own.at[pl.ds(pl.multiple_of(b * rows1, rows1), rows1)],
            gw_in.at[k],
            gw1_send.at[k],
            gw1_recv.at[k],
            blk_dev(b),
        )
        c.start()
        sends.append(c)

    for h in range(HALVES):
        for k in range(1, n_blk):
            src = blk_to(k)
            remote(
                all_h.at[h, src], all_h.at[h, src], h_send.at[h, k], h_recv.at[h, src], blk_dev(src)
            ).wait_recv()
        term[h] = jnp.dot(
            dense_t[...], all_h[h].reshape(n_blk * tile, half), preferred_element_type=F32
        ).astype(BF)
        for k in range(1, n_row):
            r = row_to(k)
            c = remote(
                term.at[h, pl.ds(pl.multiple_of(r * tile, tile), tile)],
                term_in.at[h, k],
                term_send.at[h, k],
                term_recv.at[h, k],
                row_dev(r),
            )
            c.start()
            sends.append(c)

    total = gw_own[pl.ds(pl.multiple_of(me_b * rows1, rows1), rows1), :].astype(F32)
    for k in range(1, n_blk):
        remote(
            gw_in.at[k], gw_in.at[k], gw1_send.at[k], gw1_recv.at[k], blk_dev(blk_to(k))
        ).wait_recv()
        total = total + gw_in[k].astype(F32)
    gw_sum[...] = total.astype(BF)

    owners = min(n_row, rows1 // 16)
    rows2 = rows1 // owners

    def guarded(cond, fn):
        if owners == n_row:
            fn()
        else:
            pl.when(cond)(fn)

    def slice_copy(k):
        r = row_to(k)
        return remote(
            gw_sum.at[pl.ds(pl.multiple_of(lax.rem(r, owners) * rows2, rows2), rows2)],
            gw_slice_in.at[k],
            gw2_send.at[k],
            gw2_recv.at[k],
            row_dev(r),
        )

    def spread_copy(k):
        slot = lax.rem(me_r, owners)
        return remote(
            gw_slices.at[pl.ds(pl.multiple_of(slot * rows2, rows2), rows2)],
            gw_slices.at[pl.ds(pl.multiple_of(slot * rows2, rows2), rows2)],
            gw3_send.at[k],
            gw3_recv.at[slot],
            row_dev(row_to(k)),
        )

    for k in range(1, n_row):
        guarded(row_to(k) < owners, slice_copy(k).start)

    def finish_slice():
        slot = pl.multiple_of(lax.rem(me_r, owners) * rows2, rows2)
        acc = gw_sum[pl.ds(slot, rows2), :].astype(F32)
        for k in range(1, n_row):
            slice_copy(k).wait_recv()
            acc = acc + gw_slice_in[k].astype(F32)
        gw_slices[pl.ds(slot, rows2), :] = acc.astype(BF)
        for k in range(1, n_row):
            spread_copy(k).start()

    guarded(me_r < owners, finish_slice)

    for k in range(1, n_row):
        src = row_to(k)
        slot = lax.rem(src, owners)

        def wait_slice(src=src, slot=slot, k=k):
            view = gw_slices.at[pl.ds(pl.multiple_of(slot * rows2, rows2), rows2)]
            remote(view, view, gw3_send.at[k], gw3_recv.at[slot], row_dev(src)).wait_recv()

        guarded(src < owners, wait_slice)

    for k in range(n_blk - 1, 0, -1):
        c = remote(
            gw_slices,
            gw_all.at[me_b],
            gw4_send.at[k],
            gw4_recv.at[me_b],
            blk_dev(blk_to(k)),
        )
        c.start()
        sends.append(c)
    gw_all[me_b] = gw_slices[...]

    for h in range(HALVES):
        total = term[h, pl.ds(pl.multiple_of(me_r * tile, tile), tile)].astype(F32)
        for k in range(1, n_row):
            remote(
                term_in.at[h, k], term_in.at[h, k], term_send.at[h, k], term_recv.at[h, k], row_dev(row_to(k))
            ).wait_recv()
            total = total + term_in[h, k].astype(F32)
        gf_ref[:, pl.ds(h * half, half)] = total.astype(BF)

    for k in range(1, n_blk):
        src = blk_to(k)
        remote(
            gw_all.at[src], gw_all.at[src], gw4_send.at[k], gw4_recv.at[src], blk_dev(src)
        ).wait_recv()
    gw_ref[...] = gw_all[...].reshape(wide, wide).astype(F32)

    for c in sends:
        c.wait_send()
    for k in range(1, n_row):
        guarded(row_to(k) < owners, slice_copy(k).wait_send)
    for k in range(1, n_row):
        guarded(me_r < owners, spread_copy(k).wait_send)


def on_device(features, cotangent, weight, bias, tile_values, tile_rows, tile_cols, tile_counts):
    values = tile_values[0, 0]
    n_tiles, tile = values.shape[:2]
    pieces, wide = features.shape
    n_row, n_col, n_rep = (lax.axis_size(a) for a in ("row", "col", "rep"))
    n_blk = n_col * n_rep
    row_tiles = n_blk * pieces // tile
    col_tiles = n_row * pieces // tile
    half = wide // HALVES
    rows1 = wide // n_blk
    owners = min(n_row, rows1 // 16)
    rows2 = rows1 // owners
    scale = 1.0 / math.sqrt(pieces * n_blk * n_row)
    sizes = (n_row, n_col, n_rep, n_tiles, row_tiles, col_tiles, tile, wide, scale)
    vmem = pl.BlockSpec(memory_space=pltpu.VMEM)
    smem = pl.BlockSpec(memory_space=pltpu.SMEM)
    anyw = pl.BlockSpec(memory_space=pl.ANY)
    sem = pltpu.SemaphoreType.DMA
    return pl.pallas_call(
        functools.partial(kernel, sizes),
        out_shape=(
            jax.ShapeDtypeStruct((pieces, wide), BF),
            jax.ShapeDtypeStruct((pieces, wide), BF),
            jax.ShapeDtypeStruct((wide, wide), F32),
        ),
        in_specs=[smem, smem, smem, anyw, anyw, anyw, anyw, anyw],
        out_specs=(vmem, vmem, vmem),
        scratch_shapes=[
            pltpu.VMEM((n_tiles, tile, tile), BF),
            pltpu.VMEM((row_tiles * tile, col_tiles * tile), BF),
            pltpu.VMEM((col_tiles * tile, row_tiles * tile), BF),
            pltpu.VMEM((wide, wide), BF),
            pltpu.VMEM((1, wide), F32),
            pltpu.VMEM((pieces, wide), BF),
            pltpu.VMEM((HALVES, n_row, pieces, half), BF),
            pltpu.VMEM((HALVES, n_blk * pieces, half), BF),
            pltpu.VMEM((HALVES, n_blk, pieces, half), BF),
            pltpu.VMEM((HALVES, pieces, half), BF),
            pltpu.VMEM((HALVES, n_blk, pieces, half), BF),
            pltpu.VMEM((HALVES, n_row * pieces, half), BF),
            pltpu.VMEM((HALVES, n_row, pieces, half), BF),
            pltpu.VMEM((wide, wide), BF),
            pltpu.VMEM((n_blk, rows1, wide), BF),
            pltpu.VMEM((rows1, wide), BF),
            pltpu.VMEM((n_row, rows2, wide), BF),
            pltpu.VMEM((rows1, wide), BF),
            pltpu.VMEM((n_blk, rows1, wide), BF),
            sem((4 + HALVES,)),
            sem((HALVES, n_row)),
            sem((HALVES, n_row)),
            sem((HALVES, n_blk)),
            sem((HALVES, n_blk)),
            sem((HALVES, n_blk)),
            sem((HALVES, n_blk)),
            sem((HALVES, n_row)),
            sem((HALVES, n_row)),
            sem((n_blk,)),
            sem((n_blk,)),
            sem((n_row,)),
            sem((n_row,)),
            sem((n_row,)),
            sem((n_row,)),
            sem((n_blk,)),
            sem((n_blk,)),
        ],
        compiler_params=pltpu.CompilerParams(
            collective_id=0, has_side_effects=True, vmem_limit_bytes=60 * 1024 * 1024
        ),
    )(
        tile_rows.reshape(n_tiles),
        tile_cols.reshape(n_tiles),
        tile_counts.reshape(1),
        features,
        cotangent,
        weight,
        bias.reshape(1, wide),
        values,
    )


def solution(mesh):
    placed = (
        P(("grp", "row", "col", "rep"), None),
        P(("grp", "row", "col", "rep"), None),
        P(),
        P(),
        P(("grp", "row"), ("col", "rep"), None, None, None),
        P(("grp", "row"), ("col", "rep"), None),
        P(("grp", "row"), ("col", "rep"), None),
        P(("grp", "row"), ("col", "rep")),
    )
    return jax.shard_map(
        on_device,
        mesh=mesh,
        in_specs=placed,
        out_specs=(
            P(("grp", "row", "col", "rep"), None),
            P(("grp", "row", "col", "rep"), None),
            P("grp", None),
        ),
        check_vma=False,
    )
```

```python
import functools
import math

import jax
import jax.numpy as jnp
from jax import lax
from jax.experimental import pallas as pl
from jax.experimental.pallas import tpu as pltpu
from jax.sharding import PartitionSpec as P

HALVES = 1
BF = jnp.bfloat16
F32 = jnp.float32


def kernel(
    sizes,
    rows_ref,
    cols_ref,
    count_ref,
    feat_hbm,
    cot_hbm,
    weight_hbm,
    bias_hbm,
    vals_hbm,
    act_ref,
    gf_ref,
    gw_ref,
    vals,
    dense,
    dense_t,
    weight,
    bias,
    cot,
    feats,
    part,
    part_in,
    own_g,
    all_g,
    term,
    term_in,
    gw_own,
    gw_in,
    gw_sum,
    gw_blk,
    gw_all,
    local_sem,
    feat_send,
    feat_recv,
    part_send,
    part_recv,
    g_send,
    g_recv,
    term_send,
    term_recv,
    gw1_send,
    gw1_recv,
    gw2_send,
    gw2_recv,
    gw3_send,
    gw3_recv,
):
    n_row, n_col, n_rep, n_tiles, row_tiles, col_tiles, tile, wide, scale = sizes
    n_blk = n_col * n_rep
    half = wide // HALVES
    me_r = lax.axis_index("row")
    me_c = lax.axis_index("col")
    me_p = lax.axis_index("rep")
    me_b = me_c * n_rep + me_p

    def row_to(k):
        return lax.rem(me_r + k, n_row)

    def blk_to(k):
        return lax.rem(me_c + k // n_rep, n_col) * n_rep + lax.rem(me_p + k % n_rep, n_rep)

    def row_dev(r):
        return {"row": r}

    def blk_dev(b):
        return {"col": b // n_rep, "rep": lax.rem(b, n_rep)}

    def remote(src, dst, send, recv, dev):
        return pltpu.make_async_remote_copy(
            src_ref=src,
            dst_ref=dst,
            send_sem=send,
            recv_sem=recv,
            device_id=dev,
            device_id_type=pl.DeviceIdType.MESH,
        )

    def cut(ref, h):
        return ref.at[:, pl.ds(h * half, half)]

    own_feats = [
        pltpu.make_async_copy(cut(feat_hbm, h), feats.at[h, me_r], local_sem.at[4 + h])
        for h in range(HALVES)
    ]
    load_vals = pltpu.make_async_copy(vals_hbm, vals, local_sem.at[0])
    load_weight = pltpu.make_async_copy(weight_hbm, weight, local_sem.at[1])
    load_bias = pltpu.make_async_copy(bias_hbm, bias, local_sem.at[2])
    load_cot = pltpu.make_async_copy(cot_hbm, cot, local_sem.at[3])
    for c in own_feats:
        c.start()
    load_vals.start()
    load_weight.start()
    load_bias.start()
    load_cot.start()

    barrier = pltpu.get_barrier_semaphore()
    for k in range(1, n_row):
        pl.semaphore_signal(
            barrier, inc=1, device_id=row_dev(row_to(k)), device_id_type=pl.DeviceIdType.MESH
        )
    for k in range(1, n_blk):
        pl.semaphore_signal(
            barrier, inc=1, device_id=blk_dev(blk_to(k)), device_id_type=pl.DeviceIdType.MESH
        )
    pl.semaphore_wait(barrier, n_row + n_blk - 2)

    sends = []
    for h in range(HALVES):
        for k in range(1, n_row):
            c = remote(
                cut(feat_hbm, h),
                feats.at[h, me_r],
                feat_send.at[h, k],
                feat_recv.at[h, me_r],
                row_dev(row_to(k)),
            )
            c.start()
            sends.append(c)

    load_vals.wait()
    count = count_ref[0]

    def code_of(t):
        return jnp.where(t < count, rows_ref[t] * col_tiles + cols_ref[t], -1)

    small = n_tiles * row_tiles * col_tiles <= 256
    codes = [code_of(t) for t in range(n_tiles)] if small else None

    def place(p, i, j):
        if small:
            idx = jnp.int32(-1)
            for t in range(n_tiles):
                idx = jnp.where(codes[t] == p, t, idx)
        else:
            idx = lax.fori_loop(
                0,
                n_tiles,
                lambda t, cur: jnp.where(code_of(t) == p, t, cur),
                jnp.int32(-1),
            )
        got = vals[jnp.maximum(idx, 0)]
        got = jnp.where(idx >= 0, got, jnp.zeros_like(got))
        dense[pl.ds(i * tile, tile), pl.ds(j * tile, tile)] = got
        dense_t[pl.ds(j * tile, tile), pl.ds(i * tile, tile)] = got.T

    if small:
        for p in range(row_tiles * col_tiles):
            place(p, p // col_tiles, p % col_tiles)
    else:

        def step(p, carry):
            i = p // col_tiles
            place(p, pl.multiple_of(i, 1), p - i * col_tiles)
            return carry

        lax.fori_loop(0, row_tiles * col_tiles, step, 0)

    for h in range(HALVES):
        own_feats[h].wait()
        for k in range(1, n_row):
            src = row_to(k)
            remote(
                feats.at[h, src], feats.at[h, src], feat_send.at[h, k], feat_recv.at[h, src], row_dev(src)
            ).wait_recv()
        section = feats[h].reshape(n_row * tile, half)
        part[h] = jnp.dot(dense[...], section, preferred_element_type=F32).astype(BF)
        for k in range(n_blk - 1, 0, -1):
            b = blk_to(k)
            c = remote(
                part.at[h, pl.ds(pl.multiple_of(b * tile, tile), tile)],
                part_in.at[h, k],
                part_send.at[h, k],
                part_recv.at[h, k],
                blk_dev(b),
            )
            c.start()
            sends.append(c)

    load_weight.wait()
    load_bias.wait()
    load_cot.wait()
    pre = jnp.broadcast_to(bias[...], (tile, wide))
    agg = []
    for h in range(HALVES):
        total = part[h, pl.ds(pl.multiple_of(me_b * tile, tile), tile)].astype(F32)
        for k in range(1, n_blk):
            remote(
                part_in.at[h, k], part_in.at[h, k], part_send.at[h, k], part_recv.at[h, k], blk_dev(blk_to(k))
            ).wait_recv()
            total = total + part_in[h, k].astype(F32)
        total = total.astype(BF)
        agg.append(total)
        pre = pre + jnp.dot(total, weight[pl.ds(h * half, half), :], preferred_element_type=F32)

    sig = jax.nn.sigmoid(pre)
    grad = (cot[...].astype(F32) * sig * (1.0 + pre * (1.0 - sig))).astype(BF)
    for h in range(HALVES):
        piece = grad[:, h * half : (h + 1) * half]
        own_g[h] = piece
        all_g[h, me_b] = piece
        for k in range(n_blk - 1, 0, -1):
            c = remote(
                own_g.at[h],
                all_g.at[h, me_b],
                g_send.at[h, k],
                g_recv.at[h, me_b],
                blk_dev(blk_to(k)),
            )
            c.start()
            sends.append(c)

    owners = min(n_row, wide // 16)
    rows1 = wide // owners

    def guarded(cond, fn):
        if owners == n_row:
            fn()
        else:
            pl.when(cond)(fn)

    def chunk(r):
        return pl.ds(pl.multiple_of(lax.rem(r, owners) * rows1, rows1), rows1)

    for h in range(HALVES):
        gw_own[pl.ds(h * half, half), :] = lax.dot_general(
            agg[h], grad, (((0,), (0,)), ((), ())), preferred_element_type=F32
        ).astype(BF)

    def owner_copy(k):
        r = row_to(k)
        return remote(
            gw_own.at[chunk(r)], gw_in.at[me_r], gw1_send.at[k], gw1_recv.at[me_r], row_dev(r)
        )

    def block_copy(k):
        return remote(
            gw_sum, gw_blk.at[me_b], gw2_send.at[k], gw2_recv.at[me_b], blk_dev(blk_to(k))
        )

    def final_copy(k):
        view = gw_all.at[chunk(me_r)]
        return remote(
            view, view, gw3_send.at[k], gw3_recv.at[lax.rem(me_r, owners)], row_dev(row_to(k))
        )

    for k in range(1, n_row):
        guarded(row_to(k) < owners, owner_copy(k).start)

    act_ref[...] = (pre * sig).astype(BF)

    def spread_term(h):
        term[h] = jnp.dot(
            dense_t[...], all_g[h].reshape(n_blk * tile, half), preferred_element_type=F32
        ).astype(BF)
        for k in range(1, n_row):
            r = row_to(k)
            c = remote(
                term.at[h, pl.ds(pl.multiple_of(r * tile, tile), tile)],
                term_in.at[h, k],
                term_send.at[h, k],
                term_recv.at[h, k],
                row_dev(r),
            )
            c.start()
            sends.append(c)

    for h in range(HALVES):
        for k in range(1, n_blk):
            src = blk_to(k)
            remote(
                all_g.at[h, src], all_g.at[h, src], g_send.at[h, k], g_recv.at[h, src], blk_dev(src)
            ).wait_recv()
        if h < HALVES - 1:
            spread_term(h)

    spread_term(HALVES - 1)
    def sum_rows():
        gw_in[me_r] = gw_own[chunk(me_r), :]
        for k in range(1, n_row):
            src = row_to(k)
            remote(
                gw_in.at[src], gw_in.at[src], gw1_send.at[k], gw1_recv.at[src], row_dev(src)
            ).wait_recv()
        total = gw_in[0].astype(F32)
        for r in range(1, n_row):
            total = total + gw_in[r].astype(F32)
        gw_sum[...] = total.astype(BF)
        for k in range(n_blk - 1, 0, -1):
            block_copy(k).start()

    guarded(me_r < owners, sum_rows)

    def total_chunk():
        gw_blk[me_b] = gw_sum[...]
        for k in range(1, n_blk):
            src = blk_to(k)
            remote(
                gw_blk.at[src], gw_blk.at[src], gw2_send.at[k], gw2_recv.at[src], blk_dev(src)
            ).wait_recv()
        total = gw_blk[0].astype(F32)
        for b in range(1, n_blk):
            total = total + gw_blk[b].astype(F32)
        gw_all[chunk(me_r), :] = total.astype(BF)
        for k in range(1, n_row):
            final_copy(k).start()

    guarded(me_r < owners, total_chunk)

    grad_feat = jnp.zeros((tile, wide), F32)
    for h in range(HALVES):
        total = term[h, pl.ds(pl.multiple_of(me_r * tile, tile), tile)].astype(F32)
        for k in range(1, n_row):
            remote(
                term_in.at[h, k], term_in.at[h, k], term_send.at[h, k], term_recv.at[h, k], row_dev(row_to(k))
            ).wait_recv()
            total = total + term_in[h, k].astype(F32)
        grad_feat = grad_feat + lax.dot_general(
            total.astype(BF),
            weight[:, pl.ds(h * half, half)],
            (((1,), (1,)), ((), ())),
            preferred_element_type=F32,
        )
    gf_ref[...] = grad_feat.astype(BF)

    for k in range(1, n_row):
        src = row_to(k)

        def wait_chunk(src=src, k=k):
            view = gw_all.at[chunk(src)]
            remote(
                view, view, gw3_send.at[k], gw3_recv.at[lax.rem(src, owners)], row_dev(src)
            ).wait_recv()

        guarded(src < owners, wait_chunk)
    gw_ref[...] = gw_all[...].astype(F32) * scale

    for c in sends:
        c.wait_send()
    for k in range(1, n_row):
        guarded(row_to(k) < owners, owner_copy(k).wait_send)

    def drain():
        for k in range(1, n_blk):
            block_copy(k).wait_send()
        for k in range(1, n_row):
            final_copy(k).wait_send()

    guarded(me_r < owners, drain)


def on_device(features, cotangent, weight, bias, tile_values, tile_rows, tile_cols, tile_counts):
    values = tile_values[0, 0]
    n_tiles, tile = values.shape[:2]
    pieces, wide = features.shape
    n_row, n_col, n_rep = (lax.axis_size(a) for a in ("row", "col", "rep"))
    n_blk = n_col * n_rep
    row_tiles = n_blk * pieces // tile
    col_tiles = n_row * pieces // tile
    half = wide // HALVES
    rows1 = wide // min(n_row, wide // 16)
    scale = 1.0 / math.sqrt(pieces * n_blk * n_row)
    sizes = (n_row, n_col, n_rep, n_tiles, row_tiles, col_tiles, tile, wide, scale)
    smem = pl.BlockSpec(memory_space=pltpu.SMEM)
    vmem = pl.BlockSpec(memory_space=pltpu.VMEM)
    anyw = pl.BlockSpec(memory_space=pl.ANY)
    sem = pltpu.SemaphoreType.DMA
    outs = pl.pallas_call(
        functools.partial(kernel, sizes),
        out_shape=(
            pltpu.VMEM((pieces, wide), BF),
            pltpu.VMEM((pieces, wide), BF),
            pltpu.VMEM((wide, wide), F32),
        ),
        in_specs=[smem, smem, smem, anyw, anyw, anyw, anyw, anyw],
        out_specs=(vmem, vmem, vmem),
        scratch_shapes=[
            pltpu.VMEM((n_tiles, tile, tile), BF),
            pltpu.VMEM((row_tiles * tile, col_tiles * tile), BF),
            pltpu.VMEM((col_tiles * tile, row_tiles * tile), BF),
            pltpu.VMEM((wide, wide), BF),
            pltpu.VMEM((1, wide), F32),
            pltpu.VMEM((pieces, wide), BF),
            pltpu.VMEM((HALVES, n_row, pieces, half), BF),
            pltpu.VMEM((HALVES, n_blk * pieces, half), BF),
            pltpu.VMEM((HALVES, n_blk, pieces, half), BF),
            pltpu.VMEM((HALVES, pieces, half), BF),
            pltpu.VMEM((HALVES, n_blk, pieces, half), BF),
            pltpu.VMEM((HALVES, n_row * pieces, half), BF),
            pltpu.VMEM((HALVES, n_row, pieces, half), BF),
            pltpu.VMEM((wide, wide), BF),
            pltpu.VMEM((n_row, rows1, wide), BF),
            pltpu.VMEM((rows1, wide), BF),
            pltpu.VMEM((n_blk, rows1, wide), BF),
            pltpu.VMEM((wide, wide), BF),
            sem((4 + HALVES,)),
            sem((HALVES, n_row)),
            sem((HALVES, n_row)),
            sem((HALVES, n_blk)),
            sem((HALVES, n_blk)),
            sem((HALVES, n_blk)),
            sem((HALVES, n_blk)),
            sem((HALVES, n_row)),
            sem((HALVES, n_row)),
            sem((n_row,)),
            sem((n_row,)),
            sem((n_blk,)),
            sem((n_blk,)),
            sem((n_row,)),
            sem((n_row,)),
        ],
        compiler_params=pltpu.CompilerParams(
            collective_id=0, has_side_effects=True, vmem_limit_bytes=60 * 1024 * 1024
        ),
    )(
        tile_rows.reshape(n_tiles),
        tile_cols.reshape(n_tiles),
        tile_counts.reshape(1),
        features,
        cotangent,
        weight,
        bias.reshape(1, wide),
        values,
    )
    return outs


def solution(mesh):
    placed = (
        P(("grp", "row", "col", "rep"), None),
        P(("grp", "row", "col", "rep"), None),
        P(),
        P(),
        P(("grp", "row"), ("col", "rep"), None, None, None),
        P(("grp", "row"), ("col", "rep"), None),
        P(("grp", "row"), ("col", "rep"), None),
        P(("grp", "row"), ("col", "rep")),
    )
    return jax.shard_map(
        on_device,
        mesh=mesh,
        in_specs=placed,
        out_specs=(
            P(("grp", "row", "col", "rep"), None),
            P(("grp", "row", "col", "rep"), None),
            P("grp", None),
        ),
        check_vma=False,
    )
```

```python
import functools
import math

import jax
import jax.numpy as jnp
from jax import lax
from jax.experimental import pallas as pl
from jax.experimental.pallas import tpu as pltpu
from jax.sharding import PartitionSpec as P

HALVES = 1
BF = jnp.bfloat16
F32 = jnp.float32


def kernel(
    sizes,
    rows_ref,
    cols_ref,
    count_ref,
    feat_hbm,
    cot_hbm,
    weight_hbm,
    bias_hbm,
    vals_hbm,
    act_ref,
    gf_ref,
    gw_ref,
    vals,
    dense,
    dense_t,
    weight,
    bias,
    cot,
    feats,
    part,
    part_in,
    own_g,
    all_g,
    term,
    term_in,
    gw_own,
    gw_in,
    gw_sum,
    gw_blk,
    gw_all,
    local_sem,
    feat_send,
    feat_recv,
    part_send,
    part_recv,
    g_send,
    g_recv,
    term_send,
    term_recv,
    gw1_send,
    gw1_recv,
    gw2_send,
    gw2_recv,
    gw3_send,
    gw3_recv,
    gw4_send,
    gw4_recv,
):
    n_row, n_col, n_rep, n_tiles, row_tiles, col_tiles, tile, wide, scale = sizes
    n_blk = n_col * n_rep
    half = wide // HALVES
    me_r = lax.axis_index("row")
    me_c = lax.axis_index("col")
    me_p = lax.axis_index("rep")
    me_b = me_c * n_rep + me_p

    def row_to(k):
        return lax.rem(me_r + k, n_row)

    def blk_to(k):
        return lax.rem(me_c + k // n_rep, n_col) * n_rep + lax.rem(me_p + k % n_rep, n_rep)

    def row_dev(r):
        return {"row": r}

    def blk_dev(b):
        return {"col": b // n_rep, "rep": lax.rem(b, n_rep)}

    def remote(src, dst, send, recv, dev):
        return pltpu.make_async_remote_copy(
            src_ref=src,
            dst_ref=dst,
            send_sem=send,
            recv_sem=recv,
            device_id=dev,
            device_id_type=pl.DeviceIdType.MESH,
        )

    def cut(ref, h):
        return ref.at[:, pl.ds(h * half, half)]

    own_feats = [
        pltpu.make_async_copy(cut(feat_hbm, h), feats.at[h, me_r], local_sem.at[4 + h])
        for h in range(HALVES)
    ]
    load_vals = pltpu.make_async_copy(vals_hbm, vals, local_sem.at[0])
    load_weight = pltpu.make_async_copy(weight_hbm, weight, local_sem.at[1])
    load_bias = pltpu.make_async_copy(bias_hbm, bias, local_sem.at[2])
    load_cot = pltpu.make_async_copy(cot_hbm, cot, local_sem.at[3])
    for c in own_feats:
        c.start()
    load_vals.start()
    load_weight.start()
    load_bias.start()
    load_cot.start()

    barrier = pltpu.get_barrier_semaphore()
    for k in range(1, n_row):
        pl.semaphore_signal(
            barrier, inc=1, device_id=row_dev(row_to(k)), device_id_type=pl.DeviceIdType.MESH
        )
    for k in range(1, n_blk):
        pl.semaphore_signal(
            barrier, inc=1, device_id=blk_dev(blk_to(k)), device_id_type=pl.DeviceIdType.MESH
        )
    pl.semaphore_wait(barrier, n_row + n_blk - 2)

    sends = []
    for h in range(HALVES):
        for k in range(1, n_row):
            c = remote(
                cut(feat_hbm, h),
                feats.at[h, me_r],
                feat_send.at[h, k],
                feat_recv.at[h, me_r],
                row_dev(row_to(k)),
            )
            c.start()
            sends.append(c)

    load_vals.wait()
    count = count_ref[0]

    def code_of(t):
        return jnp.where(t < count, rows_ref[t] * col_tiles + cols_ref[t], -1)

    small = n_tiles * row_tiles * col_tiles <= 256
    codes = [code_of(t) for t in range(n_tiles)] if small else None

    def place(p, i, j):
        if small:
            idx = jnp.int32(-1)
            for t in range(n_tiles):
                idx = jnp.where(codes[t] == p, t, idx)
        else:
            idx = lax.fori_loop(
                0,
                n_tiles,
                lambda t, cur: jnp.where(code_of(t) == p, t, cur),
                jnp.int32(-1),
            )
        got = vals[jnp.maximum(idx, 0)]
        got = jnp.where(idx >= 0, got, jnp.zeros_like(got))
        dense[pl.ds(i * tile, tile), pl.ds(j * tile, tile)] = got
        dense_t[pl.ds(j * tile, tile), pl.ds(i * tile, tile)] = got.T

    if small:
        for p in range(row_tiles * col_tiles):
            place(p, p // col_tiles, p % col_tiles)
    else:

        def step(p, carry):
            i = p // col_tiles
            place(p, pl.multiple_of(i, 1), p - i * col_tiles)
            return carry

        lax.fori_loop(0, row_tiles * col_tiles, step, 0)

    for h in range(HALVES):
        own_feats[h].wait()
        for k in range(1, n_row):
            src = row_to(k)
            remote(
                feats.at[h, src], feats.at[h, src], feat_send.at[h, k], feat_recv.at[h, src], row_dev(src)
            ).wait_recv()
        section = feats[h].reshape(n_row * tile, half)
        for k in range(n_blk - 1, -1, -1):
            b = blk_to(k)
            mine = pl.ds(pl.multiple_of(b * tile, tile), tile)
            part[h, mine] = jnp.dot(dense[mine, :], section, preferred_element_type=F32).astype(BF)
            if k == 0:
                break
            c = remote(
                part.at[h, pl.ds(pl.multiple_of(b * tile, tile), tile)],
                part_in.at[h, k],
                part_send.at[h, k],
                part_recv.at[h, k],
                blk_dev(b),
            )
            c.start()
            sends.append(c)

    load_weight.wait()
    load_bias.wait()
    load_cot.wait()
    pre = jnp.broadcast_to(bias[...], (tile, wide))
    agg = []
    for h in range(HALVES):
        total = part[h, pl.ds(pl.multiple_of(me_b * tile, tile), tile)].astype(F32)
        for k in range(1, n_blk):
            remote(
                part_in.at[h, k], part_in.at[h, k], part_send.at[h, k], part_recv.at[h, k], blk_dev(blk_to(k))
            ).wait_recv()
            total = total + part_in[h, k].astype(F32)
        total = total.astype(BF)
        agg.append(total)
        pre = pre + jnp.dot(total, weight[pl.ds(h * half, half), :], preferred_element_type=F32)

    sig = jax.nn.sigmoid(pre)
    grad = (cot[...].astype(F32) * sig * (1.0 + pre * (1.0 - sig))).astype(BF)
    for h in range(HALVES):
        piece = grad[:, h * half : (h + 1) * half]
        own_g[h] = piece
        all_g[h, me_b] = piece
        for k in range(n_blk - 1, 0, -1):
            c = remote(
                own_g.at[h],
                all_g.at[h, me_b],
                g_send.at[h, k],
                g_recv.at[h, me_b],
                blk_dev(blk_to(k)),
            )
            c.start()
            sends.append(c)

    owners = min(n_row, wide // 16)
    rows1 = wide // owners

    def guarded(cond, fn):
        if owners == n_row:
            fn()
        else:
            pl.when(cond)(fn)

    def chunk(r):
        return pl.ds(pl.multiple_of(lax.rem(r, owners) * rows1, rows1), rows1)

    for h in range(HALVES):
        gw_own[pl.ds(h * half, half), :] = lax.dot_general(
            agg[h], grad, (((0,), (0,)), ((), ())), preferred_element_type=F32
        ).astype(BF)

    def cols(p):
        return pl.ds(pl.multiple_of(p * (wide // n_rep), wide // n_rep), wide // n_rep)

    def core_copy(k):
        view = gw_all.at[:, cols(me_p)]
        return remote(view, view, gw4_send.at[k], gw4_recv.at[me_p], blk_dev(blk_to(k)))

    def owner_copy(k):
        r = row_to(k)
        return remote(
            gw_own.at[chunk(r)], gw_in.at[me_r], gw1_send.at[k], gw1_recv.at[me_r], row_dev(r)
        )

    def block_copy(k):
        return remote(
            gw_sum.at[:, cols(lax.rem(blk_to(k), n_rep))],
            gw_blk.at[me_b],
            gw2_send.at[k],
            gw2_recv.at[me_b],
            blk_dev(blk_to(k)),
        )

    def final_copy(k):
        view = gw_all.at[chunk(me_r), cols(me_p)]
        return remote(
            view, view, gw3_send.at[k], gw3_recv.at[lax.rem(me_r, owners)], row_dev(row_to(k))
        )

    for k in range(1, n_row):
        guarded(row_to(k) < owners, owner_copy(k).start)

    act_ref[...] = (pre * sig).astype(BF)

    def spread_term(h):
        term[h] = jnp.dot(
            dense_t[...], all_g[h].reshape(n_blk * tile, half), preferred_element_type=F32
        ).astype(BF)
        for k in range(1, n_row):
            r = row_to(k)
            c = remote(
                term.at[h, pl.ds(pl.multiple_of(r * tile, tile), tile)],
                term_in.at[h, k],
                term_send.at[h, k],
                term_recv.at[h, k],
                row_dev(r),
            )
            c.start()
            sends.append(c)

    for h in range(HALVES):
        for k in range(1, n_blk):
            src = blk_to(k)
            remote(
                all_g.at[h, src], all_g.at[h, src], g_send.at[h, k], g_recv.at[h, src], blk_dev(src)
            ).wait_recv()
        if h < HALVES - 1:
            spread_term(h)

    spread_term(HALVES - 1)
    def sum_rows():
        gw_in[me_r] = gw_own[chunk(me_r), :]
        for k in range(1, n_row):
            src = row_to(k)
            remote(
                gw_in.at[src], gw_in.at[src], gw1_send.at[k], gw1_recv.at[src], row_dev(src)
            ).wait_recv()
        total = gw_in[0].astype(F32)
        for r in range(1, n_row):
            total = total + gw_in[r].astype(F32)
        gw_sum[...] = total.astype(BF)
        for k in range(n_blk - 1, 0, -1):
            block_copy(k).start()

    guarded(me_r < owners, sum_rows)

    def total_chunk():
        gw_blk[me_b] = gw_sum[:, cols(me_p)]
        for k in range(1, n_blk):
            src = blk_to(k)
            remote(
                gw_blk.at[src], gw_blk.at[src], gw2_send.at[k], gw2_recv.at[src], blk_dev(src)
            ).wait_recv()
        total = gw_blk[0].astype(F32)
        for b in range(1, n_blk):
            total = total + gw_blk[b].astype(F32)
        gw_all[chunk(me_r), cols(me_p)] = total.astype(BF)
        for k in range(1, n_row):
            final_copy(k).start()

    guarded(me_r < owners, total_chunk)

    for k in range(1, n_row):
        src = row_to(k)

        def wait_chunk(src=src, k=k):
            view = gw_all.at[chunk(src), cols(me_p)]
            remote(
                view, view, gw3_send.at[k], gw3_recv.at[lax.rem(src, owners)], row_dev(src)
            ).wait_recv()

        guarded(src < owners, wait_chunk)
    for k in range(1, n_rep):
        core_copy(k).start()

    grad_feat = jnp.zeros((tile, wide), F32)
    for h in range(HALVES):
        total = term[h, pl.ds(pl.multiple_of(me_r * tile, tile), tile)].astype(F32)
        for k in range(1, n_row):
            remote(
                term_in.at[h, k], term_in.at[h, k], term_send.at[h, k], term_recv.at[h, k], row_dev(row_to(k))
            ).wait_recv()
            total = total + term_in[h, k].astype(F32)
        grad_feat = grad_feat + lax.dot_general(
            total.astype(BF),
            weight[:, pl.ds(h * half, half)],
            (((1,), (1,)), ((), ())),
            preferred_element_type=F32,
        )
    gf_ref[...] = grad_feat.astype(BF)

    for k in range(1, n_rep):
        p = lax.rem(me_p + k, n_rep)
        view = gw_all.at[:, cols(p)]
        remote(view, view, gw4_send.at[k], gw4_recv.at[p], blk_dev(blk_to(k))).wait_recv()
    gw_ref[...] = gw_all[...].astype(F32) * scale

    for c in sends:
        c.wait_send()
    for k in range(1, n_rep):
        core_copy(k).wait_send()
    for k in range(1, n_row):
        guarded(row_to(k) < owners, owner_copy(k).wait_send)

    def drain():
        for k in range(1, n_blk):
            block_copy(k).wait_send()
        for k in range(1, n_row):
            final_copy(k).wait_send()

    guarded(me_r < owners, drain)


def on_device(features, cotangent, weight, bias, tile_values, tile_rows, tile_cols, tile_counts):
    values = tile_values[0, 0]
    n_tiles, tile = values.shape[:2]
    pieces, wide = features.shape
    n_row, n_col, n_rep = (lax.axis_size(a) for a in ("row", "col", "rep"))
    n_blk = n_col * n_rep
    row_tiles = n_blk * pieces // tile
    col_tiles = n_row * pieces // tile
    half = wide // HALVES
    rows1 = wide // min(n_row, wide // 16)
    scale = 1.0 / math.sqrt(pieces * n_blk * n_row)
    sizes = (n_row, n_col, n_rep, n_tiles, row_tiles, col_tiles, tile, wide, scale)
    smem = pl.BlockSpec(memory_space=pltpu.SMEM)
    vmem = pl.BlockSpec(memory_space=pltpu.VMEM)
    anyw = pl.BlockSpec(memory_space=pl.ANY)
    sem = pltpu.SemaphoreType.DMA
    outs = pl.pallas_call(
        functools.partial(kernel, sizes),
        out_shape=(
            pltpu.VMEM((pieces, wide), BF),
            pltpu.VMEM((pieces, wide), BF),
            pltpu.VMEM((wide, wide), F32),
        ),
        in_specs=[smem, smem, smem, anyw, anyw, anyw, anyw, anyw],
        out_specs=(vmem, vmem, vmem),
        scratch_shapes=[
            pltpu.VMEM((n_tiles, tile, tile), BF),
            pltpu.VMEM((row_tiles * tile, col_tiles * tile), BF),
            pltpu.VMEM((col_tiles * tile, row_tiles * tile), BF),
            pltpu.VMEM((wide, wide), BF),
            pltpu.VMEM((1, wide), F32),
            pltpu.VMEM((pieces, wide), BF),
            pltpu.VMEM((HALVES, n_row, pieces, half), BF),
            pltpu.VMEM((HALVES, n_blk * pieces, half), BF),
            pltpu.VMEM((HALVES, n_blk, pieces, half), BF),
            pltpu.VMEM((HALVES, pieces, half), BF),
            pltpu.VMEM((HALVES, n_blk, pieces, half), BF),
            pltpu.VMEM((HALVES, n_row * pieces, half), BF),
            pltpu.VMEM((HALVES, n_row, pieces, half), BF),
            pltpu.VMEM((wide, wide), BF),
            pltpu.VMEM((n_row, rows1, wide), BF),
            pltpu.VMEM((rows1, wide), BF),
            pltpu.VMEM((n_blk, rows1, wide // n_rep), BF),
            pltpu.VMEM((wide, wide), BF),
            sem((4 + HALVES,)),
            sem((HALVES, n_row)),
            sem((HALVES, n_row)),
            sem((HALVES, n_blk)),
            sem((HALVES, n_blk)),
            sem((HALVES, n_blk)),
            sem((HALVES, n_blk)),
            sem((HALVES, n_row)),
            sem((HALVES, n_row)),
            sem((n_row,)),
            sem((n_row,)),
            sem((n_blk,)),
            sem((n_blk,)),
            sem((n_row,)),
            sem((n_row,)),
            sem((n_rep,)),
            sem((n_rep,)),
        ],
        compiler_params=pltpu.CompilerParams(
            collective_id=0, has_side_effects=True, vmem_limit_bytes=60 * 1024 * 1024
        ),
    )(
        tile_rows.reshape(n_tiles),
        tile_cols.reshape(n_tiles),
        tile_counts.reshape(1),
        features,
        cotangent,
        weight,
        bias.reshape(1, wide),
        values,
    )
    return outs


def solution(mesh):
    placed = (
        P(("grp", "row", "col", "rep"), None),
        P(("grp", "row", "col", "rep"), None),
        P(),
        P(),
        P(("grp", "row"), ("col", "rep"), None, None, None),
        P(("grp", "row"), ("col", "rep"), None),
        P(("grp", "row"), ("col", "rep"), None),
        P(("grp", "row"), ("col", "rep")),
    )
    return jax.shard_map(
        on_device,
        mesh=mesh,
        in_specs=placed,
        out_specs=(
            P(("grp", "row", "col", "rep"), None),
            P(("grp", "row", "col", "rep"), None),
            P("grp", None),
        ),
        check_vma=False,
    )
```
